256 devices in a mesh: batch: 16 (over x, z_lo, core), row: 4 (over z_hi), col: 4 (over y).
Axes of the slice: x: 4, y: 4, z: 8 (z_hi: 4, z_lo: 2; z = z_hi * 2 + z_lo), core: 2. Of those that a mesh axis runs over, the one named last changes fastest.
Arguments:
- view_one: bfloat16 [2048, 8192], P('batch', ('row', 'col')), may hold values from -20 to 20, as said below
- view_two: bfloat16 [2048, 8192], P('batch', ('row', 'col')), may hold values from -20 to 20, as said below
Outputs:
- grad_one: bfloat16 [2048, 8192], P('batch', ('row', 'col'))
- grad_two: bfloat16 [2048, 8192], P('batch', ('row', 'col'))
The draws below stay inside these ranges and needn't reach their ends.
Inputs may be any that keep to these rules, and one draw needn't show every extreme that they name: `view_one`: projector outputs; features differ in scale. `view_two`: projector outputs; features differ in scale.
All inputs are finite; a program needn't handle non-finite values.
Results may differ from the reference program's by a relative error of at most 0.0051.
Values may be sent and summed in bfloat16 or wider, within the bound.
No kernel may reach another device: no remote copies, remote signals or barrier semaphores. Data moves between devices by JAX's collectives and lax.ppermute only.
A program may use at most 128 MiB of HBM per device.

```python
import math
import jax
import jax.numpy as jnp
from jax import lax

D = 8192
SAMPLES = 2048


def feature_scale(key):
    picked = jax.random.uniform(jax.random.fold_in(key, 11), (D,))
    lower = jax.random.uniform(jax.random.fold_in(key, 12), (D,), minval=math.log(0.3), maxval=math.log(0.8))
    upper = jax.random.uniform(jax.random.fold_in(key, 13), (D,), minval=math.log(1.25), maxval=math.log(3.0))
    return jnp.exp(jnp.where(picked < 0.5, lower, upper))


def sample_scale(low_end, high_end):
    position = jnp.arange(SAMPLES, dtype=jnp.float32) / (SAMPLES - 1)
    return jnp.exp(math.log(low_end) + position * (math.log(high_end) - math.log(low_end)))


def shared_normal(key):
    common = jax.random.normal(jax.random.fold_in(key, 14), (SAMPLES, D))
    offset = 0.1 * jax.random.normal(jax.random.fold_in(key, 15), (D,))
    return (feature_scale(key), common, offset)


def draw_view_one(key, part):
    scale, common, offset = shared_normal(key)
    rows = sample_scale(0.6, 1.8)
    key = jax.random.fold_in(key, 1)
    own_part = jax.random.normal(key, (SAMPLES, D))
    return jnp.clip(rows[:, None] * scale * (0.8 * common + 0.6 * own_part + offset), -20.0, 20.0).astype(jnp.bfloat16)


def draw_view_two(key, part):
    scale, common, offset = shared_normal(key)
    rows = sample_scale(0.6, 1.8)
    key = jax.random.fold_in(key, 2)
    own_part = jax.random.normal(key, (SAMPLES, D))
    return jnp.clip(rows[:, None] * scale * (0.8 * common + 0.6 * own_part + offset), -20.0, 20.0).astype(jnp.bfloat16)


def setup_inputs(seed: int = 0) -> dict:
    arg_keys = jax.random.split(jax.random.key(seed), 3)
    return {
        "view_one": draw_view_one(jax.random.fold_in(arg_keys[2], 71), 0),
        "view_two": draw_view_two(jax.random.fold_in(arg_keys[2], 71), 0),
    }


def covariance_product(rounded, sample_count):
    block_width = math.gcd(D, 512)
    block_count = D // block_width

    def one_block(first_col):
        columns = lax.dynamic_slice_in_dim(rounded, first_col, block_width, 1)
        cov_block = jnp.dot(rounded.T, columns, preferred_element_type=jnp.float32) / (sample_count - 1)
        row_ids = jnp.arange(D, dtype=jnp.int32)[:, None]
        col_ids = first_col + jnp.arange(block_width, dtype=jnp.int32)[None, :]
        cov_block = jnp.where(row_ids == col_ids, jnp.zeros_like(cov_block), cov_block).astype(jnp.bfloat16)
        return jnp.dot(rounded, cov_block, preferred_element_type=jnp.float32)
    starts = jnp.arange(block_count, dtype=jnp.int32) * block_width
    blocks = lax.map(one_block, starts)
    return jnp.transpose(blocks, (1, 0, 2)).reshape(rounded.shape[0], D)

def statistics(values, sample_count):
    mean_val = lax.optimization_barrier(jnp.sum(values, axis=0)) / sample_count
    centered = values - mean_val
    variance = lax.optimization_barrier(jnp.sum(centered * centered, axis=0)) / (sample_count - 1)
    std_val = jnp.sqrt(variance + 0.0001)
    hinge = jnp.where(std_val < 1.0, 1.0 / std_val, jnp.zeros_like(std_val))
    return (centered, hinge)

def reference(view_one, view_two):
    sample_count = view_one.shape[0]
    first_view = view_one.astype(jnp.float32)
    second_view = view_two.astype(jnp.float32)
    cent_one, hinge_one = statistics(first_view, sample_count)
    cent_two, hinge_two = statistics(second_view, sample_count)
    product_one = covariance_product(cent_one.astype(jnp.bfloat16), sample_count)
    product_two = covariance_product(cent_two.astype(jnp.bfloat16), sample_count)
    coef_var = sample_count / (2.0 * (sample_count - 1))
    coef_cov = 2.0 * sample_count / (25.0 * (sample_count - 1))
    grad_one = first_view - second_view - coef_var * hinge_one * cent_one + coef_cov * product_one
    grad_two = second_view - first_view - coef_var * hinge_two * cent_two + coef_cov * product_two
    return (grad_one.astype(jnp.bfloat16), grad_two.astype(jnp.bfloat16))
```

```python
import jax
import jax.numpy as jnp
from jax import lax
from jax.sharding import PartitionSpec as P

BF = jnp.bfloat16
F32 = jnp.float32


def hinge_of(variance):
    std_val = jnp.sqrt(variance + 0.0001)
    return jnp.where(std_val < 1.0, 1.0 / std_val, jnp.zeros_like(std_val))


def swap(x, bit):
    return lax.ppermute(x, "batch", [(i, i ^ bit) for i in range(lax.axis_size("batch"))])


def partner(place, core, turn):
    return place ^ 1 if turn == core else 3 - place


def exchange(x, axis, turn, same=False):
    groups, size = lax.axis_size("batch"), lax.axis_size(axis)
    pairs = [
        (b * size + i, b * size + partner(i, 0 if same else b % 2, turn))
        for b in range(groups)
        for i in range(size)
    ]
    return lax.ppermute(x, ("batch", axis), pairs)


def move(x, places, flip=0):
    pairs = [
        (b, ((b // 4 + places) % 4 * 4 + b % 4) ^ (2 * flip))
        for b in range(lax.axis_size("batch"))
    ]
    return lax.ppermute(x, "batch", pairs)


def scatter_sum(parts, axis, send):
    keep = parts[:2] + exchange(send, axis, 0).astype(F32)
    return keep[0] + exchange(keep[1].astype(BF), axis, 1).astype(F32)


def gather_pair(x, axis):
    return jnp.concatenate([x, exchange(x, axis, 1, same=True)], axis=0)


def full_sum(x, axis):
    for turn in (0, 1):
        x = x + exchange(x.astype(BF), axis, turn).astype(F32)
    return x


def ordered(x, axis, turned, back=False):
    place = lax.axis_index(axis)
    high = place // 2
    low = high ^ (place % 2)
    x = x.reshape((2, 2) + x.shape[1:])
    if back:
        x = jnp.where(turned, x.swapaxes(0, 1), x)
    x = jnp.where(high == 1, x[::-1], x)
    x = jnp.where(low == 1, x[:, ::-1], x)
    if not back:
        x = jnp.where(turned, x.swapaxes(0, 1), x)
    return x.reshape((4,) + x.shape[2:])


def on_device(view_one, view_two):
    local_rows, width = view_one.shape
    groups = lax.axis_size("batch")
    sample_count = local_rows * groups
    place = lax.axis_index("batch")
    first = place // 2 % 2 == 0
    core = place % 2
    other = jnp.where(first, view_two, view_one)
    mine = jnp.where(first, view_one, view_two)
    away, away_far = move(other, 0, flip=1), move(other, 2, flip=1)
    low, high = move(mine, 1), move(mine, -1)
    near = jnp.concatenate([mine, low, away, move(away, 1)], axis=0)
    rest = jnp.concatenate([high, move(away, -1), move(high, -1), away_far], axis=0)
    full = jnp.concatenate([near, rest, swap(near, 1), swap(rest, 1)], axis=0)
    mean_val = jnp.sum(full.astype(F32), axis=0, keepdims=True) / sample_count
    rounded = (full.astype(F32) - mean_val).astype(BF)
    coef_var = sample_count / (2.0 * (sample_count - 1))
    coef_cov = 2.0 * sample_count / (25.0 * (sample_count - 1) * (sample_count - 1))
    quarter = local_rows // 4

    def gram_of(raw, earlier=None):
        own_cent = raw.astype(F32) - mean_val
        own = own_cent.astype(BF)
        blocks = ordered(own.reshape(4, quarter, width), "col", core == 0).reshape(local_rows, width)
        if earlier is not None:
            blocks, earlier = lax.optimization_barrier((blocks, earlier))
        gram = jnp.dot(blocks, rounded.T, preferred_element_type=F32)
        parts = gram.reshape(4, quarter, sample_count)
        return parts, parts[2:].astype(BF)

    def term_of(raw):
        own_cent = raw.astype(F32) - mean_late
        own = own_cent.astype(BF)
        return own.astype(F32) * feature_squares * coef_cov + coef_var * hinge * own_cent

    def pair_of(parts, send):
        total = full_sum(scatter_sum(parts, "col", send), "row").astype(BF)
        return gather_pair(total, "col")

    def away_part(rows, term):
        return (coef_cov * jnp.dot(rows, rounded, preferred_element_type=F32) - term).astype(BF)

    parts_away, send_away = gram_of(away)
    parts_mine, send_mine = gram_of(mine, send_away)
    full_late, mean_late, away_late, mine_late, _ = lax.optimization_barrier(
        (full, mean_val, away, mine, send_mine)
    )
    cent = full_late.astype(F32) - mean_late
    variance = jnp.sum(cent * cent, axis=0, keepdims=True) / (sample_count - 1)
    hinge = hinge_of(variance)
    wide = cent.astype(BF).astype(F32)
    feature_squares = jnp.sum(wide * wide, axis=0, keepdims=True)
    term_away, term_mine = term_of(away_late), term_of(mine_late)
    term_away = ordered(term_away.reshape(4, quarter, width), "col", True)
    term_away = term_away.reshape(2, 2 * quarter, width)
    pair_away = pair_of(parts_away, send_away)
    wide_away = exchange(pair_away, "col", 0, same=True)
    early = away_part(pair_away, term_away[0])
    late = away_part(wide_away, term_away[1])
    extra_other = jnp.concatenate([swap(early, 2), swap(late, 2)], axis=0)
    extra_other = extra_other.astype(F32).reshape(4, quarter, width)
    extra_other = ordered(extra_other, "col", True, back=True).reshape(local_rows, width)
    pair_mine = pair_of(parts_mine, send_mine)
    wide_mine = exchange(pair_mine, "col", 0, same=True)
    whole, _ = lax.optimization_barrier((jnp.concatenate([pair_mine, wide_mine], axis=0), late))
    product = jnp.dot(whole, rounded, preferred_element_type=F32)
    product = ordered(product.reshape(4, quarter, width), "col", True, back=True)
    extra_mine = coef_cov * product.reshape(local_rows, width) - term_mine
    diff = view_one.astype(F32) - view_two.astype(F32)
    grad_one = diff + jnp.where(first, extra_mine, extra_other)
    grad_two = jnp.where(first, extra_other, extra_mine) - diff
    return (grad_one.astype(BF), grad_two.astype(BF))


def solution(mesh):
    in_specs = (P("batch", ("row", "col")), P("batch", ("row", "col")))
    out_specs = (P("batch", ("row", "col")), P("batch", ("row", "col")))
    return jax.shard_map(
        on_device, mesh=mesh, in_specs=in_specs, out_specs=out_specs, check_vma=False
    )
```

```python
import jax
import jax.numpy as jnp
from jax import lax
from jax.sharding import PartitionSpec as P

BF = jnp.bfloat16
F32 = jnp.float32


def hinge_of(variance):
    std_val = jnp.sqrt(variance + 0.0001)
    return jnp.where(std_val < 1.0, 1.0 / std_val, jnp.zeros_like(std_val))


def swap(x, bit):
    return lax.ppermute(x, "batch", [(i, i ^ bit) for i in range(lax.axis_size("batch"))])


def partner(place, core, turn):
    return place ^ 1 if turn == core else 3 - place


def exchange(x, axis, turn, same=False):
    groups, size = lax.axis_size("batch"), lax.axis_size(axis)
    pairs = [
        (b * size + i, b * size + partner(i, 0 if same else b % 2, turn))
        for b in range(groups)
        for i in range(size)
    ]
    return lax.ppermute(x, ("batch", axis), pairs)


def move(x, places, flip=0):
    pairs = [
        (b, ((b // 4 + places) % 4 * 4 + b % 4) ^ (2 * flip))
        for b in range(lax.axis_size("batch"))
    ]
    return lax.ppermute(x, "batch", pairs)


def scatter_sum(parts, axis, send):
    keep = parts[:2] + exchange(send, axis, 0).astype(F32)
    return keep[0] + exchange(keep[1].astype(BF), axis, 1).astype(F32)


def gather_pair(x, axis):
    return jnp.concatenate([x, exchange(x, axis, 1, same=True)], axis=0)


def full_sum(x, axis):
    for turn in (0, 1):
        x = x + exchange(x.astype(BF), axis, turn).astype(F32)
    return x


def ordered(x, axis, turned, back=False):
    place = lax.axis_index(axis)
    high = place // 2
    low = high ^ (place % 2)
    x = x.reshape((2, 2) + x.shape[1:])
    if back:
        x = jnp.where(turned, x.swapaxes(0, 1), x)
    x = jnp.where(high == 1, x[::-1], x)
    x = jnp.where(low == 1, x[:, ::-1], x)
    if not back:
        x = jnp.where(turned, x.swapaxes(0, 1), x)
    return x.reshape((4,) + x.shape[2:])


def on_device(view_one, view_two):
    local_rows, width = view_one.shape
    groups = lax.axis_size("batch")
    sample_count = local_rows * groups
    place = lax.axis_index("batch")
    first = place // 2 % 2 == 0
    core = place % 2
    other = jnp.where(first, view_two, view_one)
    mine = jnp.where(first, view_one, view_two)
    away, away_far = move(other, 0, flip=1), move(other, 2, flip=1)
    low, high = move(mine, 1), move(mine, -1)
    near = jnp.concatenate([mine, low, away, move(away, 1)], axis=0)
    rest = jnp.concatenate([high, move(away, -1), move(high, -1), away_far], axis=0)
    full = jnp.concatenate([near, rest, swap(near, 1), swap(rest, 1)], axis=0)
    mean_val = jnp.sum(full.astype(F32), axis=0, keepdims=True) / sample_count
    rounded = (full.astype(F32) - mean_val).astype(BF)
    coef_var = sample_count / (2.0 * (sample_count - 1))
    coef_cov = 2.0 * sample_count / (25.0 * (sample_count - 1) * (sample_count - 1))
    quarter = local_rows // 4

    def gram_of(raw, earlier=None):
        own_cent = raw.astype(F32) - mean_val
        own = own_cent.astype(BF)
        blocks = ordered(own.reshape(4, quarter, width), "col", core == 0).reshape(local_rows, width)
        if earlier is not None:
            blocks, earlier = lax.optimization_barrier((blocks, earlier))
        gram = jnp.dot(blocks, rounded.T, preferred_element_type=F32)
        parts = gram.reshape(4, quarter, sample_count)
        return parts, parts[2:].astype(BF)

    def term_of(raw):
        own_cent = raw.astype(F32) - mean_late
        own = own_cent.astype(BF)
        return own.astype(F32) * feature_squares * coef_cov + coef_var * hinge * own_cent

    def pair_of(parts, send):
        total = full_sum(scatter_sum(parts, "col", send), "row").astype(BF)
        return gather_pair(total, "col")

    def away_part(rows, term):
        return (coef_cov * jnp.dot(rows, rounded, preferred_element_type=F32) - term).astype(BF)

    parts_away, send_away = gram_of(away)
    parts_mine, send_mine = gram_of(mine, send_away)
    full_late, mean_late, away_late, mine_late, _ = lax.optimization_barrier(
        (full, mean_val, away, mine, send_mine)
    )
    cent = full_late.astype(F32) - mean_late
    variance = jnp.sum(cent * cent, axis=0, keepdims=True) / (sample_count - 1)
    hinge = hinge_of(variance)
    wide = cent.astype(BF).astype(F32)
    feature_squares = jnp.sum(wide * wide, axis=0, keepdims=True)
    term_away, term_mine = term_of(away_late), term_of(mine_late)
    term_away = ordered(term_away.reshape(4, quarter, width), "col", True)
    term_away = term_away.reshape(2, 2 * quarter, width)
    pair_away = pair_of(parts_away, send_away)
    wide_away = exchange(pair_away, "col", 0, same=True)
    early = away_part(pair_away, term_away[0])
    late = away_part(wide_away, term_away[1])
    extra_other = jnp.concatenate([swap(early, 2), swap(late, 2)], axis=0)
    extra_other = extra_other.astype(F32).reshape(4, quarter, width)
    extra_other = ordered(extra_other, "col", True, back=True).reshape(local_rows, width)
    pair_mine = pair_of(parts_mine, send_mine)
    wide_mine = exchange(pair_mine, "col", 0, same=True)
    whole, _ = lax.optimization_barrier((jnp.concatenate([pair_mine, wide_mine], axis=0), late))
    product = jnp.dot(whole, rounded, preferred_element_type=F32)
    product = ordered(product.reshape(4, quarter, width), "col", True, back=True)
    extra_mine = coef_cov * product.reshape(local_rows, width) - term_mine
    diff = mine.astype(F32) - other.astype(F32)
    grad_mine, grad_other = diff + extra_mine, extra_other - diff
    grad_one = jnp.where(first, grad_mine, grad_other)
    grad_two = jnp.where(first, grad_other, grad_mine)
    return (grad_one.astype(BF), grad_two.astype(BF))


def solution(mesh):
    in_specs = (P("batch", ("row", "col")), P("batch", ("row", "col")))
    out_specs = (P("batch", ("row", "col")), P("batch", ("row", "col")))
    return jax.shard_map(
        on_device, mesh=mesh, in_specs=in_specs, out_specs=out_specs, check_vma=False
    )
```

```python
import jax
import jax.numpy as jnp
from jax import lax
from jax.sharding import PartitionSpec as P

BF = jnp.bfloat16
F32 = jnp.float32


def hinge_of(variance):
    std_val = jnp.sqrt(variance + 0.0001)
    return jnp.where(std_val < 1.0, 1.0 / std_val, jnp.zeros_like(std_val))


def swap(x, bit):
    return lax.ppermute(x, "batch", [(i, i ^ bit) for i in range(lax.axis_size("batch"))])


def partner(place, core, turn):
    return place ^ 1 if turn == core else 3 - place


def exchange(x, axis, turn, same=False):
    groups, size = lax.axis_size("batch"), lax.axis_size(axis)
    pairs = [
        (b * size + i, b * size + partner(i, 0 if same else b % 2, turn))
        for b in range(groups)
        for i in range(size)
    ]
    return lax.ppermute(x, ("batch", axis), pairs)


def move(x, places, flip=0):
    pairs = [
        (b, ((b // 4 + places) % 4 * 4 + b % 4) ^ (2 * flip))
        for b in range(lax.axis_size("batch"))
    ]
    return lax.ppermute(x, "batch", pairs)


def scatter_sum(parts, axis, send):
    keep = parts[:2] + exchange(send, axis, 0).astype(F32)
    return keep[0] + exchange(keep[1].astype(BF), axis, 1).astype(F32)


def gather_pair(x, axis, same):
    return jnp.concatenate([x, exchange(x, axis, 1, same=same)], axis=0)


def full_sum(x, axis):
    for turn in (0, 1):
        x = x + exchange(x.astype(BF), axis, turn).astype(F32)
    return x


def ordered(x, axis, turned, back=False):
    place = lax.axis_index(axis)
    high = place // 2
    low = high ^ (place % 2)
    x = x.reshape((2, 2) + x.shape[1:])
    if back:
        x = jnp.where(turned, x.swapaxes(0, 1), x)
    x = jnp.where(high == 1, x[::-1], x)
    x = jnp.where(low == 1, x[:, ::-1], x)
    if not back:
        x = jnp.where(turned, x.swapaxes(0, 1), x)
    return x.reshape((4,) + x.shape[2:])


def on_device(view_one, view_two):
    local_rows, width = view_one.shape
    groups = lax.axis_size("batch")
    sample_count = local_rows * groups
    place = lax.axis_index("batch")
    first = place // 2 % 2 == 0
    core = place % 2
    other = jnp.where(first, view_two, view_one)
    mine = jnp.where(first, view_one, view_two)
    away, away_far = move(other, 0, flip=1), move(other, 2, flip=1)
    low, high = move(mine, 1), move(mine, -1)
    onward = move(jnp.concatenate([away, high], axis=0), -1)
    near = jnp.concatenate([mine, low, away, move(away, 1)], axis=0)
    rest = jnp.concatenate([high, onward, away_far], axis=0)
    full = jnp.concatenate([near, rest, swap(near, 1), swap(rest, 1)], axis=0)
    mean_val = jnp.sum(full.astype(F32), axis=0, keepdims=True) / sample_count
    rounded = (full.astype(F32) - mean_val).astype(BF)
    coef_var = sample_count / (2.0 * (sample_count - 1))
    coef_cov = 2.0 * sample_count / (25.0 * (sample_count - 1) * (sample_count - 1))
    quarter = local_rows // 4

    def gram_of(raw, earlier=None):
        own_cent = raw.astype(F32) - mean_val
        own = own_cent.astype(BF)
        blocks = ordered(own.reshape(4, quarter, width), "col", core == 0).reshape(local_rows, width)
        if earlier is not None:
            blocks, earlier = lax.optimization_barrier((blocks, earlier))
        gram = jnp.dot(blocks, rounded.T, preferred_element_type=F32)
        parts = gram.reshape(4, quarter, sample_count)
        return parts, parts[2:].astype(BF)

    def term_of(raw):
        own_cent = raw.astype(F32) - mean_late
        own = own_cent.astype(BF)
        return own.astype(F32) * feature_squares * coef_cov + coef_var * hinge * own_cent

    def pair_of(parts, send, same):
        total = full_sum(scatter_sum(parts, "col", send), "row").astype(BF)
        return gather_pair(total, "col", same)

    def away_part(rows, term):
        return (coef_cov * jnp.dot(rows, rounded, preferred_element_type=F32) - term).astype(BF)

    parts_away, send_away = gram_of(away)
    parts_mine, send_mine = gram_of(mine, send_away)
    full_late, mean_late, away_late, mine_late, _ = lax.optimization_barrier(
        (full, mean_val, away, mine, send_mine)
    )
    cent = full_late.astype(F32) - mean_late
    variance = jnp.sum(cent * cent, axis=0, keepdims=True) / (sample_count - 1)
    hinge = hinge_of(variance)
    wide = cent.astype(BF).astype(F32)
    feature_squares = jnp.sum(wide * wide, axis=0, keepdims=True)
    term_away, term_mine = term_of(away_late), term_of(mine_late)
    term_away = ordered(term_away.reshape(4, quarter, width), "col", True)
    term_away = term_away.reshape(2, 2 * quarter, width)
    pair_away = pair_of(parts_away, send_away, True)
    wide_away = exchange(pair_away, "col", 0, same=True)
    early = away_part(pair_away, term_away[0])
    late = away_part(wide_away, term_away[1])
    extra_other = jnp.concatenate([swap(early, 2), swap(late, 2)], axis=0)
    extra_other = extra_other.astype(F32).reshape(4, quarter, width)
    extra_other = ordered(extra_other, "col", True, back=True).reshape(local_rows, width)
    pair_mine = pair_of(parts_mine, send_mine, False)
    wide_mine = exchange(pair_mine, "col", 0)
    whole, _ = lax.optimization_barrier((jnp.concatenate([pair_mine, wide_mine], axis=0), late))
    product = jnp.dot(whole, rounded, preferred_element_type=F32)
    product = ordered(product.reshape(4, quarter, width), "col", core == 0, back=True)
    extra_mine = coef_cov * product.reshape(local_rows, width) - term_mine
    diff = mine.astype(F32) - other.astype(F32)
    grad_mine, grad_other = diff + extra_mine, extra_other - diff
    grad_one = jnp.where(first, grad_mine, grad_other)
    grad_two = jnp.where(first, grad_other, grad_mine)
    return (grad_one.astype(BF), grad_two.astype(BF))


def solution(mesh):
    in_specs = (P("batch", ("row", "col")), P("batch", ("row", "col")))
    out_specs = (P("batch", ("row", "col")), P("batch", ("row", "col")))
    return jax.shard_map(
        on_device, mesh=mesh, in_specs=in_specs, out_specs=out_specs, check_vma=False
    )
```

```python
import jax
import jax.numpy as jnp
from jax import lax
from jax.sharding import PartitionSpec as P

BF = jnp.bfloat16
F32 = jnp.float32


def hinge_of(variance):
    std_val = jnp.sqrt(variance + 0.0001)
    return jnp.where(std_val < 1.0, 1.0 / std_val, jnp.zeros_like(std_val))


def swap(x, bit):
    return lax.ppermute(x, "batch", [(i, i ^ bit) for i in range(lax.axis_size("batch"))])


def partner(place, core, turn):
    return place ^ 1 if turn == core else 3 - place


def exchange(x, axis, turn, same=False):
    groups, size = lax.axis_size("batch"), lax.axis_size(axis)
    pairs = [
        (b * size + i, b * size + partner(i, 0 if same else b % 2, turn))
        for b in range(groups)
        for i in range(size)
    ]
    return lax.ppermute(x, ("batch", axis), pairs)


def move(x, places, flip=0):
    pairs = [
        (b, ((b // 4 + places) % 4 * 4 + b % 4) ^ (2 * flip))
        for b in range(lax.axis_size("batch"))
    ]
    return lax.ppermute(x, "batch", pairs)


def scatter_sum(parts, axis, send):
    keep = parts[:2] + exchange(send, axis, 0).astype(F32)
    return keep[0] + exchange(keep[1].astype(BF), axis, 1).astype(F32)


def gather_pair(x, axis):
    return jnp.concatenate([x, exchange(x, axis, 1, same=True)], axis=0)


def full_sum(x, axis):
    for turn in (0, 1):
        x = x + exchange(x.astype(BF), axis, turn).astype(F32)
    return x


def ordered(x, axis, turned, back=False):
    place = lax.axis_index(axis)
    high = place // 2
    low = high ^ (place % 2)
    x = x.reshape((2, 2) + x.shape[1:])
    if back:
        x = jnp.where(turned, x.swapaxes(0, 1), x)
    x = jnp.where(high == 1, x[::-1], x)
    x = jnp.where(low == 1, x[:, ::-1], x)
    if not back:
        x = jnp.where(turned, x.swapaxes(0, 1), x)
    return x.reshape((4,) + x.shape[2:])


def on_device(view_one, view_two):
    local_rows, width = view_one.shape
    groups = lax.axis_size("batch")
    sample_count = local_rows * groups
    place = lax.axis_index("batch")
    first = place // 2 % 2 == 0
    core = place % 2
    other = jnp.where(first, view_two, view_one)
    mine = jnp.where(first, view_one, view_two)
    away, away_far = move(other, 0, flip=1), move(other, 2, flip=1)
    low, high = move(mine, 1), move(mine, -1)
    onward = move(jnp.concatenate([away, high], axis=0), -1)
    near = jnp.concatenate([mine, low, away, move(away, 1)], axis=0)
    rest = jnp.concatenate([high, onward, away_far], axis=0)
    full = jnp.concatenate([near, rest, swap(near, 1), swap(rest, 1)], axis=0)
    mean_val = jnp.sum(full.astype(F32), axis=0, keepdims=True) / sample_count
    rounded = (full.astype(F32) - mean_val).astype(BF)
    coef_var = sample_count / (2.0 * (sample_count - 1))
    coef_cov = 2.0 * sample_count / (25.0 * (sample_count - 1) * (sample_count - 1))
    quarter = local_rows // 4

    own = [(raw.astype(F32) - mean_val).astype(BF) for raw in (away, mine)]
    blocks = [ordered(x.reshape(4, quarter, width), "col", core == 0) for x in own]
    blocks = jnp.concatenate(blocks, axis=0).reshape(2 * local_rows, width)
    gram = jnp.dot(blocks, rounded.T, preferred_element_type=F32)
    parts_away, parts_mine = gram.reshape(2, 4, quarter, sample_count)
    send_away, send_mine = parts_away[2:].astype(BF), parts_mine[2:].astype(BF)

    def term_of(raw):
        own_cent = raw.astype(F32) - mean_late
        own = own_cent.astype(BF)
        return own.astype(F32) * feature_squares * coef_cov + coef_var * hinge * own_cent

    def pair_of(parts, send):
        total = full_sum(scatter_sum(parts, "col", send), "row").astype(BF)
        return gather_pair(total, "col")

    def away_part(rows, term):
        return (coef_cov * jnp.dot(rows, rounded, preferred_element_type=F32) - term).astype(BF)

    full_late, mean_late, away_late, mine_late, _ = lax.optimization_barrier(
        (full, mean_val, away, mine, send_away)
    )
    cent = full_late.astype(F32) - mean_late
    variance = jnp.sum(cent * cent, axis=0, keepdims=True) / (sample_count - 1)
    hinge = hinge_of(variance)
    wide = cent.astype(BF).astype(F32)
    feature_squares = jnp.sum(wide * wide, axis=0, keepdims=True)
    send_mine, feature_squares = lax.optimization_barrier((send_mine, feature_squares))
    term_away, term_mine = term_of(away_late), term_of(mine_late)
    term_away = ordered(term_away.reshape(4, quarter, width), "col", True)
    term_away = term_away.reshape(2, 2 * quarter, width)
    pair_away = pair_of(parts_away, send_away)
    wide_away = exchange(pair_away, "col", 0, same=True)
    early = away_part(pair_away, term_away[0])
    late = away_part(wide_away, term_away[1])
    extra_other = jnp.concatenate([swap(early, 2), swap(late, 2)], axis=0)
    extra_other = extra_other.astype(F32).reshape(4, quarter, width)
    extra_other = ordered(extra_other, "col", True, back=True).reshape(local_rows, width)
    pair_mine = pair_of(parts_mine, send_mine)
    wide_mine = exchange(pair_mine, "col", 0, same=True)
    whole, _ = lax.optimization_barrier((jnp.concatenate([pair_mine, wide_mine], axis=0), late))
    product = jnp.dot(whole, rounded, preferred_element_type=F32)
    product = ordered(product.reshape(4, quarter, width), "col", True, back=True)
    extra_mine = coef_cov * product.reshape(local_rows, width) - term_mine
    diff = mine.astype(F32) - other.astype(F32)
    grad_mine, grad_other = diff + extra_mine, extra_other - diff
    grad_one = jnp.where(first, grad_mine, grad_other)
    grad_two = jnp.where(first, grad_other, grad_mine)
    return (grad_one.astype(BF), grad_two.astype(BF))


def solution(mesh):
    in_specs = (P("batch", ("row", "col")), P("batch", ("row", "col")))
    out_specs = (P("batch", ("row", "col")), P("batch", ("row", "col")))
    return jax.shard_map(
        on_device, mesh=mesh, in_specs=in_specs, out_specs=out_specs, check_vma=False
    )
```

```python
import jax
import jax.numpy as jnp
from jax import lax
from jax.sharding import PartitionSpec as P

BF = jnp.bfloat16
F32 = jnp.float32


def hinge_of(variance):
    std_val = jnp.sqrt(variance + 0.0001)
    return jnp.where(std_val < 1.0, 1.0 / std_val, jnp.zeros_like(std_val))


def swap(x, bit):
    return lax.ppermute(x, "batch", [(i, i ^ bit) for i in range(lax.axis_size("batch"))])


def partner(place, core, turn):
    return place ^ 1 if turn == core else 3 - place


def exchange(x, axis, turn, same=False):
    groups, size = lax.axis_size("batch"), lax.axis_size(axis)
    pairs = [
        (b * size + i, b * size + partner(i, 0 if same else b % 2, turn))
        for b in range(groups)
        for i in range(size)
    ]
    return lax.ppermute(x, ("batch", axis), pairs)


def move(x, places, flip=0):
    pairs = [
        (b, ((b // 4 + places) % 4 * 4 + b % 4) ^ (2 * flip))
        for b in range(lax.axis_size("batch"))
    ]
    return lax.ppermute(x, "batch", pairs)


def scatter_sum(parts, axis, send):
    keep = parts[:2] + exchange(send, axis, 0).astype(F32)
    return keep[0] + exchange(keep[1].astype(BF), axis, 1).astype(F32)


def gather_pair(x, axis):
    return jnp.concatenate([x, exchange(x, axis, 1, same=True)], axis=0)


def full_sum(x, axis):
    for turn in (0, 1):
        x = x + exchange(x.astype(BF), axis, turn).astype(F32)
    return x


def ordered(x, axis, turned, back=False):
    place = lax.axis_index(axis)
    high = place // 2
    low = high ^ (place % 2)
    x = x.reshape((2, 2) + x.shape[1:])
    if back:
        x = jnp.where(turned, x.swapaxes(0, 1), x)
    x = jnp.where(high == 1, x[::-1], x)
    x = jnp.where(low == 1, x[:, ::-1], x)
    if not back:
        x = jnp.where(turned, x.swapaxes(0, 1), x)
    return x.reshape((4,) + x.shape[2:])


def on_device(view_one, view_two):
    local_rows, width = view_one.shape
    groups = lax.axis_size("batch")
    sample_count = local_rows * groups
    place = lax.axis_index("batch")
    first = place // 2 % 2 == 0
    core = place % 2
    other = jnp.where(first, view_two, view_one)
    mine = jnp.where(first, view_one, view_two)
    away, away_far = move(other, 0, flip=1), move(other, 2, flip=1)
    low, high = move(mine, 1), move(mine, -1)
    near = jnp.concatenate([mine, low, away, move(away, 1)], axis=0)
    rest = jnp.concatenate([high, move(away, -1), move(high, -1), away_far], axis=0)
    full = jnp.concatenate([near, rest, swap(near, 1), swap(rest, 1)], axis=0)
    mean_val = jnp.sum(full.astype(F32), axis=0, keepdims=True) / sample_count
    rounded = (full.astype(F32) - mean_val).astype(BF)
    coef_var = sample_count / (2.0 * (sample_count - 1))
    coef_cov = 2.0 * sample_count / (25.0 * (sample_count - 1) * (sample_count - 1))
    quarter = local_rows // 4

    own = [(raw.astype(F32) - mean_val).astype(BF) for raw in (away, mine)]
    blocks = [ordered(x.reshape(4, quarter, width), "col", core == 0) for x in own]
    blocks = jnp.concatenate(blocks, axis=0).reshape(2 * local_rows, width)
    gram = jnp.dot(blocks, rounded.T, preferred_element_type=F32)
    parts_away, parts_mine = gram.reshape(2, 4, quarter, sample_count)
    send_away, send_mine = parts_away[2:].astype(BF), parts_mine[2:].astype(BF)

    def term_of(raw):
        own_cent = raw.astype(F32) - mean_late
        own = own_cent.astype(BF)
        return own.astype(F32) * feature_squares * coef_cov + coef_var * hinge * own_cent

    def pair_of(parts, send):
        total = full_sum(scatter_sum(parts, "col", send), "row").astype(BF)
        return gather_pair(total, "col")

    def away_part(rows, term):
        return (coef_cov * jnp.dot(rows, rounded, preferred_element_type=F32) - term).astype(BF)

    full_late, mean_late, away_late, mine_late, _ = lax.optimization_barrier(
        (full, mean_val, away, mine, send_away)
    )
    cent = full_late.astype(F32) - mean_late
    variance = jnp.sum(cent * cent, axis=0, keepdims=True) / (sample_count - 1)
    hinge = hinge_of(variance)
    wide = cent.astype(BF).astype(F32)
    feature_squares = jnp.sum(wide * wide, axis=0, keepdims=True)
    send_mine, feature_squares = lax.optimization_barrier((send_mine, feature_squares))
    term_away, term_mine = term_of(away_late), term_of(mine_late)
    term_away = ordered(term_away.reshape(4, quarter, width), "col", True)
    term_away = term_away.reshape(2, 2 * quarter, width)
    pair_away = pair_of(parts_away, send_away)
    wide_away = exchange(pair_away, "col", 0, same=True)
    early = away_part(pair_away, term_away[0])
    late = away_part(wide_away, term_away[1])
    extra_other = jnp.concatenate([swap(early, 2), swap(late, 2)], axis=0)
    extra_other = extra_other.astype(F32).reshape(4, quarter, width)
    extra_other = ordered(extra_other, "col", True, back=True).reshape(local_rows, width)
    pair_mine = pair_of(parts_mine, send_mine)
    wide_mine = exchange(pair_mine, "col", 0, same=True)
    whole, _ = lax.optimization_barrier((jnp.concatenate([pair_mine, wide_mine], axis=0), late))
    product = jnp.dot(whole, rounded, preferred_element_type=F32)
    product = ordered(product.reshape(4, quarter, width), "col", True, back=True)
    extra_mine = coef_cov * product.reshape(local_rows, width) - term_mine
    diff = mine.astype(F32) - other.astype(F32)
    grad_mine, grad_other = diff + extra_mine, extra_other - diff
    grad_one = jnp.where(first, grad_mine, grad_other)
    grad_two = jnp.where(first, grad_other, grad_mine)
    return (grad_one.astype(BF), grad_two.astype(BF))


def solution(mesh):
    in_specs = (P("batch", ("row", "col")), P("batch", ("row", "col")))
    out_specs = (P("batch", ("row", "col")), P("batch", ("row", "col")))
    return jax.shard_map(
        on_device, mesh=mesh, in_specs=in_specs, out_specs=out_specs, check_vma=False
    )
```

```python
import jax
import jax.numpy as jnp
from jax import lax
from jax.sharding import PartitionSpec as P

BF = jnp.bfloat16
F32 = jnp.float32


def hinge_of(variance):
    std_val = jnp.sqrt(variance + 0.0001)
    return jnp.where(std_val < 1.0, 1.0 / std_val, jnp.zeros_like(std_val))


def swap(x, bit):
    return lax.ppermute(x, "batch", [(i, i ^ bit) for i in range(lax.axis_size("batch"))])


def partner(place, core, turn):
    return place ^ 1 if turn == core else 3 - place


def exchange(x, axis, turn, same=False):
    groups, size = lax.axis_size("batch"), lax.axis_size(axis)
    pairs = [
        (b * size + i, b * size + partner(i, 0 if same else b % 2, turn))
        for b in range(groups)
        for i in range(size)
    ]
    return lax.ppermute(x, ("batch", axis), pairs)


def move(x, places, flip=0):
    pairs = [
        (b, ((b // 4 + places) % 4 * 4 + b % 4) ^ (2 * flip))
        for b in range(lax.axis_size("batch"))
    ]
    return lax.ppermute(x, "batch", pairs)


def scatter_sum(parts, axis, send):
    keep = parts[:2] + exchange(send, axis, 0).astype(F32)
    return keep[0] + exchange(keep[1].astype(BF), axis, 1).astype(F32)


def gather_pair(x, axis):
    return jnp.concatenate([x, exchange(x, axis, 1, same=True)], axis=0)


def full_sum(x, axis):
    for turn in (0, 1):
        x = x + exchange(x.astype(BF), axis, turn).astype(F32)
    return x


def ordered(x, axis, turned, back=False):
    place = lax.axis_index(axis)
    high = place // 2
    low = high ^ (place % 2)
    x = x.reshape((2, 2) + x.shape[1:])
    if back:
        x = jnp.where(turned, x.swapaxes(0, 1), x)
    x = jnp.where(high == 1, x[::-1], x)
    x = jnp.where(low == 1, x[:, ::-1], x)
    if not back:
        x = jnp.where(turned, x.swapaxes(0, 1), x)
    return x.reshape((4,) + x.shape[2:])


def on_device(view_one, view_two):
    local_rows, width = view_one.shape
    groups = lax.axis_size("batch")
    sample_count = local_rows * groups
    place = lax.axis_index("batch")
    first = place // 2 % 2 == 0
    core = place % 2
    other = jnp.where(first, view_two, view_one)
    mine = jnp.where(first, view_one, view_two)
    away, away_far = move(other, 0, flip=1), move(other, 2, flip=1)
    low, high = move(mine, 1), move(mine, -1)
    onward = move(jnp.concatenate([away, high], axis=0), -1)
    near = jnp.concatenate([mine, low, away, move(away, 1)], axis=0)
    rest = jnp.concatenate([high, onward, away_far], axis=0)
    full = jnp.concatenate([near, rest, swap(near, 1), swap(rest, 1)], axis=0)
    mean_val = jnp.sum(full.astype(F32), axis=0, keepdims=True) / sample_count
    rounded = (full.astype(F32) - mean_val).astype(BF)
    coef_var = sample_count / (2.0 * (sample_count - 1))
    coef_cov = 2.0 * sample_count / (25.0 * (sample_count - 1) * (sample_count - 1))
    quarter = local_rows // 4

    own = [(raw.astype(F32) - mean_val).astype(BF) for raw in (away, mine)]
    blocks = [ordered(x.reshape(4, quarter, width), "col", core == 0) for x in own]
    blocks = jnp.concatenate(blocks, axis=0).reshape(2 * local_rows, width)
    gram = jnp.dot(blocks, rounded.T, preferred_element_type=F32)
    parts_away, parts_mine = gram.reshape(2, 4, quarter, sample_count)
    send_away, send_mine = parts_away[2:].astype(BF), parts_mine[2:].astype(BF)

    def term_of(raw):
        own_cent = raw.astype(F32) - mean_late
        own = own_cent.astype(BF)
        return own.astype(F32) * feature_squares * coef_cov + coef_var * hinge * own_cent

    def pair_of(parts, send):
        total = full_sum(scatter_sum(parts, "col", send), "row").astype(BF)
        return gather_pair(total, "col")

    def away_part(rows, term):
        return (coef_cov * jnp.dot(rows, rounded, preferred_element_type=F32) - term).astype(BF)

    full_late, mean_late, away_late, mine_late, _ = lax.optimization_barrier(
        (full, mean_val, away, mine, send_away)
    )
    cent = full_late.astype(F32) - mean_late
    variance = jnp.sum(cent * cent, axis=0, keepdims=True) / (sample_count - 1)
    hinge = hinge_of(variance)
    wide = cent.astype(BF).astype(F32)
    feature_squares = jnp.sum(wide * wide, axis=0, keepdims=True)
    term_away, term_mine = term_of(away_late), term_of(mine_late)
    term_away = ordered(term_away.reshape(4, quarter, width), "col", True)
    term_away = term_away.reshape(2, 2 * quarter, width)
    pair_away = pair_of(parts_away, send_away)
    wide_away = exchange(pair_away, "col", 0, same=True)
    early = away_part(pair_away, term_away[0])
    late = away_part(wide_away, term_away[1])
    extra_other = jnp.concatenate([swap(early, 2), swap(late, 2)], axis=0)
    extra_other = extra_other.astype(F32).reshape(4, quarter, width)
    extra_other = ordered(extra_other, "col", True, back=True).reshape(local_rows, width)
    pair_mine = pair_of(parts_mine, send_mine)
    wide_mine = exchange(pair_mine, "col", 0, same=True)
    whole, _ = lax.optimization_barrier((jnp.concatenate([pair_mine, wide_mine], axis=0), late))
    product = jnp.dot(whole, rounded, preferred_element_type=F32)
    product = ordered(product.reshape(4, quarter, width), "col", True, back=True)
    extra_mine = coef_cov * product.reshape(local_rows, width) - term_mine
    diff = mine.astype(F32) - other.astype(F32)
    grad_mine, grad_other = diff + extra_mine, extra_other - diff
    grad_one = jnp.where(first, grad_mine, grad_other)
    grad_two = jnp.where(first, grad_other, grad_mine)
    return (grad_one.astype(BF), grad_two.astype(BF))


def solution(mesh):
    in_specs = (P("batch", ("row", "col")), P("batch", ("row", "col")))
    out_specs = (P("batch", ("row", "col")), P("batch", ("row", "col")))
    return jax.shard_map(
        on_device, mesh=mesh, in_specs=in_specs, out_specs=out_specs, check_vma=False
    )
```
